512 devices in a mesh: blk: 128 (over x, z, y_hi, core), aux: 4 (over y_lo).
Axes of the slice: x: 4, y: 8 (y_hi: 2, y_lo: 4; y = y_hi * 4 + y_lo), z: 8, core: 2. Of those that a mesh axis runs over, the one named last changes fastest.
Arguments:
- factors: bfloat16 [2, 3584, 10240], P(None, 'blk', 'aux'), may hold values from -0.0625 to 0.0625
- amplitudes: bfloat16 [8, 3584, 3584], P(None, 'blk'), may hold values from -0.09375 to 0.09375
Outputs:
- ladder: float32 [8, 2, 2], replicated
The draws below stay inside these ranges and needn't reach their ends.
All inputs are finite; a program needn't handle non-finite values.
Results may differ from the reference program's by a relative error of at most 0.0003.
Values may be sent and summed in bfloat16 or wider, within the bound.
A program may use at most 64 MiB of HBM per device.

```python
import math
import jax
import jax.numpy as jnp
from jax import lax

V = 3584
Q = 10240
PAIRS = 8
A = 2


def block_levels(rng, shape, pieces, low, top_value):
    gain = 1.0
    for dim, shards_of in pieces:
        draws = jax.random.uniform(jax.random.fold_in(jax.random.fold_in(rng, 6), dim), (shards_of,), jnp.float32, low / len(pieces), top_value / len(pieces))
        gain = gain * jnp.repeat(jnp.exp(draws), shape[dim] // shards_of).reshape((-1,) + (1,) * (len(shape) - 1 - dim))
    return gain


def centred(key, dims, scale, most, split=(), kind=jnp.bfloat16):
    loudness = block_levels(key, dims, split, -0.22, 0.18) if split else 1.0
    array = jax.random.normal(key, dims, jnp.float32) * scale * loudness
    return jnp.minimum(jnp.maximum(array, -most), most).astype(kind)


def setup_inputs(seed: int = 0) -> dict:
    splits = jax.random.split(jax.random.key(seed), 3)
    factors = centred(splits[0], (A, V, Q), Q ** -0.5, 0.0625, ((1, 128), (2, 4)))
    amplitudes = centred(splits[1], (PAIRS, V, V), V ** -0.5, 0.09375, ((1, 128),))
    return {"factors": factors, "amplitudes": amplitudes}


def reference(factors, amplitudes):
    block_len = math.gcd(V, 512)
    widened = factors.astype(jnp.float32)

    def one_block(start):
        slab_rows = lax.dynamic_slice_in_dim(widened, start, block_len, 1)
        integrals = jnp.einsum("acq,bdq->acbd", slab_rows, widened, precision=lax.Precision.HIGHEST)
        amp_block = lax.dynamic_slice_in_dim(amplitudes, start, block_len, 1).astype(jnp.float32)
        return jnp.einsum("acbd,pcd->pab", integrals, amp_block, precision=lax.Precision.HIGHEST)

    starts = jnp.arange(V // block_len, dtype=jnp.int32) * block_len
    return jnp.sum(lax.map(one_block, starts), axis=0)
```

```python
import jax
import jax.numpy as jnp
from jax import lax
from jax.experimental import pallas as pl
from jax.experimental.pallas import tpu as pltpu
from jax.sharding import PartitionSpec as P

MESH = pl.DeviceIdType.MESH
F32, BF16 = jnp.float32, jnp.bfloat16

NX, NZ, NL = 4, 8, 4
BL = 28
W = 2 * BL
ROWS = 2 * W
PADDED = 128
HALF = 1280
CHUNK = HALF // 2
SLAB = NZ * 2 * W
PK = 4
TROWS = PK * W
WIN1 = (0, 128, 384, 512)
NT = (((1,), (1,)), ((), ()))
PEERS = 21


def dot(a, b):
    return jnp.dot(a, b, preferred_element_type=F32)


def one_hot(rows, columns, test):
    r = lax.broadcasted_iota(jnp.int32, (rows, columns), 0)
    c = lax.broadcasted_iota(jnp.int32, (rows, columns), 1)
    return jnp.where(test(r, c), 1.0, 0.0).astype(BF16)


class Ring:
    def __init__(self, n, pos, slot, device, send, recv):
        self.n, self.pos, self.slot, self.device, self.send, self.recv = n, pos, slot, device, send, recv
        self.steps = n - 1

    def copy(self, way, step, back):
        q = step % 2 if way == 0 else 1 - step % 2
        j = step // 2 + back
        block = lax.rem(self.pos + (self.n - j if way == 0 else j), self.n)
        ref = self.slot(q, block)
        to = lax.rem(self.pos + (1 if way == 0 else self.n - 1), self.n)
        return pltpu.make_async_remote_copy(
            src_ref=ref,
            dst_ref=ref,
            send_sem=self.send.at[way, step],
            recv_sem=self.recv.at[way, step],
            device_id=self.device(to),
            device_id_type=MESH,
        )

    def start(self, way, step):
        self.copy(way, step, 0).start()

    def step(self, step):
        for way in (0, 1):
            self.copy(way, step, 1).wait_recv()
            if step + 2 < self.steps:
                self.start(way, step + 2)

    def finish(self):
        for step in range(self.steps):
            for way in (0, 1):
                self.copy(way, step, 0).wait_send()


def kernel(
    f_hbm, t_hbm, out_ref,
    fm, fo, df, tm, to, tf, tb, zb, xh, xo, p1, v2, t1, t2, s1, ex, iscr, tex, acc, red0, red1, red2,
    loc, cs, cr, zs, zr, xs, xr, os, orr, ys, yr, p1s, p1r, p2s, p2r, ls, lr, c1s, c1r, c2s, c2r, rs, rr,
):
    blk = lax.axis_index("blk")
    l = lax.axis_index("aux")
    k = lax.rem(blk, 2)
    h = lax.rem(lax.div(blk, 2), 2)
    z = lax.rem(lax.div(blk, 4), NZ)
    x = lax.div(blk, 4 * NZ)
    m = lax.rem(l, 2)

    def at(x_, z_, h_, k_, l_):
        return (((x_ * NZ + z_) * 2 + h_) * 2 + k_, l_)

    other_core = at(x, z, h, 1 - k, l)
    other_half = at(x, z, 1 - h, k, l)
    partner = at(x, z, h, k, l + 1 - 2 * m)

    def xk_peer(o):
        g = lax.rem(x * 2 + k + o, 8)
        return at(lax.div(g, 2), z, h, lax.rem(g, 2), l)

    def z_peer(o):
        return at(x, lax.rem(z + o, NZ), h, k, l)

    def y_peer(o):
        g = lax.rem(h * NL + l + o, 8)
        return at(x, z, lax.div(g, NL), k, lax.rem(g, NL))

    def remote(src, dst, send, recv, device):
        return pltpu.make_async_remote_copy(
            src_ref=src, dst_ref=dst, send_sem=send, recv_sem=recv, device_id=device, device_id_type=MESH
        )

    own_q = pl.multiple_of(k * HALF, 128)
    other_q = pl.multiple_of((1 - k) * HALF, 128)
    load_f = pltpu.make_async_copy(f_hbm.at[:, :, pl.ds(own_q, HALF)], fm, loc.at[0])
    load_t = pltpu.make_async_copy(t_hbm.at[pl.ds(PK * k, PK)], tm, loc.at[1])
    load_f.start()
    load_t.start()

    barrier = pltpu.get_barrier_semaphore()
    for o in range(1, 8):
        for peer in (xk_peer(o), z_peer(o), y_peer(o)):
            pl.semaphore_signal(barrier, inc=1, device_id=peer, device_id_type=MESH)

    zero = jnp.zeros((PADDED - ROWS, CHUNK), BF16)
    for q in range(2):
        for i in range(NZ):
            zb[q, i, pl.ds(ROWS, PADDED - ROWS), :] = zero
        for i in range(NX):
            xo[q, i, pl.ds(ROWS, PADDED - ROWS), :] = zero
    acc[...] = jnp.zeros_like(acc)
    for i in range(4):
        s1[i] = one_hot(
            384, 128, lambda r, c: ((c % 64) < W) & (r == (2 * i + c // 64) * 2 * W + h * W + c % 64 - WIN1[i])
        )
    for i in range(2):
        ex[i] = one_hot(
            128, 128, lambda r, c: (c < 2 * W) & (r == 64 * i + jnp.where(c < W, c, c - W))
        )

    pl.semaphore_wait(barrier, PEERS)

    swap_f = remote(f_hbm.at[:, :, pl.ds(other_q, HALF)], fo, cs.at[0], cr.at[0], other_core)
    swap_t = remote(t_hbm.at[pl.ds(PK * (1 - k), PK)], to, cs.at[1], cr.at[1], other_core)
    swap_f.start()
    swap_t.start()

    load_f.wait()
    swap_f.wait_recv()
    for a in range(2):
        for kk in range(2):
            df[pl.ds(a * W + kk * BL, BL), :] = jnp.where(k == kk, fm[a].astype(F32), fo[a].astype(F32))
    for q in range(2):
        chunk = df[:, q * CHUNK : (q + 1) * CHUNK].astype(BF16)
        zb[q, z, pl.ds(0, ROWS), :] = chunk
        xh[q, x] = chunk

    ring_z = Ring(NZ, z, lambda q, i: zb.at[q, i, pl.ds(0, ROWS)], lambda i: at(x, i, h, k, l), zs, zr)
    ring_x = Ring(NX, x, lambda q, i: xh.at[q, i], lambda i: at(i, z, h, k, l), xs, xr)
    ring_o = Ring(NX, x, lambda q, i: xo.at[q, i, pl.ds(0, ROWS)], lambda i: at(i, z, h, k, l), os, orr)

    def swap_y(q):
        return remote(xh.at[q, x], xo.at[q, x, pl.ds(0, ROWS)], ys.at[q], yr.at[q], other_half)

    for step in range(2):
        for way in (0, 1):
            ring_z.start(way, step)
        for way in (0, 1):
            ring_x.start(way, step)
        swap_y(step).start()

    load_t.wait()
    swap_t.wait_recv()
    for s in range(NX):
        for p in range(PK):
            for kk in range(2):
                mine = tm[p, :, s * SLAB : (s + 1) * SLAB].astype(F32)
                theirs = to[p, :, s * SLAB : (s + 1) * SLAB].astype(F32)
                tf[pl.ds(p * W + kk * BL, BL), :] = jnp.where(k == kk, mine, theirs)
        tb[s] = tf[...].astype(BF16)

    def send_p1(o):
        to_x = lax.rem(x + o, NX)
        return remote(p1.at[to_x], t1.at[k, x], p1s.at[o], p1r.at[o], at(to_x, z, h, k, l))

    def send_p2(o):
        to_z = lax.rem(z + o, NZ)
        return remote(v2.at[to_z], t2.at[k, z, m], p2s.at[o], p2r.at[o], at(x, to_z, h, k, l))

    for s in range(NX):
        for i in range(4):
            p1[s, i] = dot(tb[s, :, WIN1[i] : WIN1[i] + 384], s1[i]).astype(BF16)
    for o in range(1, NX):
        send_p1(o).start()
    for i in range(NZ):
        first = min(128 * (i * 2 * W // 128), SLAB - 256)
        base = i * 2 * W - first
        low = one_hot(256, 128, lambda r, c: (c < W) & (r == base + (1 - h) * W + c))
        high = one_hot(256, 128, lambda r, c: (c >= 64) & (c < 64 + W) & (r == base + (1 - h) * W + c - 64))
        v2[i] = (
            dot(tb[2 * m, :, first : first + 256], low) + dot(tb[2 * m + 1, :, first : first + 256], high)
        ).astype(BF16)
    for o in range(1, NZ):
        send_p2(o).start()
    t1[k, x] = p1[x]
    t2[k, z, m] = v2[z]

    def t1_forward(o):
        ref = t1.at[k, lax.rem(x + NX - o, NX)]
        return remote(ref, ref, c1s.at[o], c1r.at[o], other_core)

    def t1_arrived(o):
        ref = t1.at[1 - k, lax.rem(x + NX - o, NX)]
        return remote(ref, ref, c1s.at[o], c1r.at[o], other_core)

    def p1_arrived(o):
        ref = t1.at[k, lax.rem(x + NX - o, NX)]
        return remote(ref, ref, p1s.at[o], p1r.at[o], other_core)

    def p2_arrived(o):
        ref = t2.at[k, lax.rem(z + NZ - o, NZ), m]
        return remote(ref, ref, p2s.at[o], p2r.at[o], other_core)

    def t2_share(o):
        ref = t2.at[k, lax.rem(z + NZ - o, NZ), m]
        return remote(ref, ref, ls.at[o], lr.at[o], partner)

    def share_arrived(o):
        ref = t2.at[k, lax.rem(z + NZ - o, NZ), 1 - m]
        return remote(ref, ref, ls.at[o], lr.at[o], partner)

    def t2_forward(o, part):
        ref = t2.at[k, lax.rem(z + NZ - o, NZ), m if part == 0 else 1 - m]
        return remote(ref, ref, c2s.at[part, o], c2r.at[part, o], other_core)

    def t2_arrived(o, part):
        ref = t2.at[1 - k, lax.rem(z + NZ - o, NZ), m if part == 0 else 1 - m]
        return remote(ref, ref, c2s.at[part, o], c2r.at[part, o], other_core)

    t1_forward(0).start()
    t2_share(0).start()
    t2_forward(0, 0).start()

    def multiply(block, tiles, which):
        spread = ex[which]
        for kk in range(2):
            tex[pl.ds(kk * TROWS, TROWS), :] = dot(tiles(kk), spread)
        i0 = iscr[pl.ds(pl.multiple_of(block * ROWS, 8), W), :]
        i1 = iscr[pl.ds(pl.multiple_of(block * ROWS + W, 8), W), :]
        for p in range(2 * PK):
            t = tex[pl.ds(p * W, W), :]
            acc[2 * p] += jnp.sum((i0 * t).reshape(W // 8, 8, 128), axis=0)
            acc[2 * p + 1] += jnp.sum((i1 * t).reshape(W // 8, 8, 128), axis=0)

    def own_half(o):
        zi = lax.rem(z + o, NZ)
        total = 0.0
        for q in range(2):
            total += lax.dot_general(
                xh[q].reshape(NX * ROWS, CHUNK), zb[q, zi], NT, preferred_element_type=F32
            )
        iscr[...] = total

        def body(b, _):
            multiply(b, lambda kk: t1[kk, b, lax.div(zi, 2)], lax.rem(zi, 2))
            return 0

        lax.fori_loop(0, NX, body, 0)

    def cross_half(offsets):
        zis = [lax.rem(z + o, NZ) for o in offsets]

        def body(b, _):
            total = 0.0
            for q in range(2):
                rows = jnp.concatenate([zb[q, zi, pl.ds(0, ROWS), :] for zi in zis], axis=0)
                total += lax.dot_general(rows, xo[q, b], NT, preferred_element_type=F32)
            iscr[...] = total
            for i, zi in enumerate(zis):
                multiply(i, lambda kk: t2[kk, zi, lax.div(b, 2)], lax.rem(b, 2))
            return 0

        lax.fori_loop(0, NX, body, 0)

    ring_z.step(0)
    ring_x.step(0)
    ring_z.step(1)
    ring_x.step(1)
    ring_z.step(2)
    ring_x.step(2)
    swap_y(0).wait_recv()
    ring_o.start(0, 0)
    ring_o.start(1, 1)
    ring_z.step(3)
    swap_y(1).wait_recv()
    ring_o.start(0, 1)
    ring_o.start(1, 0)
    for o in range(1, NX):
        p1_arrived(o).wait_recv()
        t1_forward(o).start()
    ring_z.step(4)
    ring_o.step(0)
    for o in range(NX):
        t1_arrived(o).wait_recv()
    own_half(0)
    ring_z.step(5)
    ring_o.step(1)
    for o in (1, 7):
        own_half(o)
    ring_z.step(6)
    ring_o.step(2)

    def pass_on(o, _):
        p2_arrived(o).wait_recv()
        t2_share(o).start()
        t2_forward(o, 0).start()
        return 0

    lax.fori_loop(1, NZ, pass_on, 0)
    for o in (2, 6, 3, 5, 4):
        own_half(o)

    def pass_shared(o, _):
        share_arrived(o).wait_recv()
        t2_forward(o, 1).start()
        return 0

    lax.fori_loop(0, NZ, pass_shared, 0)

    def settle(o, _):
        t2_arrived(o, 0).wait_recv()
        t2_arrived(o, 1).wait_recv()
        return 0

    lax.fori_loop(0, NZ, settle, 0)
    cross_half((0, 1, 7, 2))
    cross_half((6, 3, 5, 4))

    total = jnp.sum(acc[...], axis=1)
    for i, (held, me, peer) in enumerate(
        ((red0, x * 2 + k, xk_peer), (red1, z, z_peer), (red2, h * NL + l, y_peer))
    ):
        held[me] = total
        for o in range(1, 8):
            remote(held.at[me], held.at[me], rs.at[i, o], rr.at[i, o], peer(o)).start()
        for o in range(1, 8):
            ref = held.at[lax.rem(me + 8 - o, 8)]
            remote(ref, ref, rs.at[i, o], rr.at[i, o], peer(o)).wait_recv()
        total = held[0]
        for o in range(1, 8):
            total = total + held[o]
    lane = lax.broadcasted_iota(jnp.int32, total.shape, 1)
    b0 = jnp.sum(jnp.where(lane < W, total, 0.0), axis=1, keepdims=True)
    b1 = jnp.sum(jnp.where(lane < W, 0.0, total), axis=1, keepdims=True)
    both = jnp.where(lax.broadcasted_iota(jnp.int32, (16, 2), 1) == 0, b0, b1)
    for p in range(2 * PK):
        out_ref[p] = both[2 * p : 2 * p + 2, :]

    swap_f.wait_send()
    swap_t.wait_send()
    ring_z.finish()
    ring_x.finish()
    ring_o.finish()
    for q in range(2):
        swap_y(q).wait_send()
    for o in range(1, NX):
        send_p1(o).wait_send()
    for o in range(NX):
        t1_forward(o).wait_send()
    for o in range(1, NZ):
        send_p2(o).wait_send()
    for o in range(NZ):
        t2_share(o).wait_send()
        t2_forward(o, 0).wait_send()
        t2_forward(o, 1).wait_send()
    for i, (held, me, peer) in enumerate(
        ((red0, x * 2 + k, xk_peer), (red1, z, z_peer), (red2, h * NL + l, y_peer))
    ):
        for o in range(1, 8):
            remote(held.at[me], held.at[me], rs.at[i, o], rr.at[i, o], peer(o)).wait_send()


def shards(factors, amplitudes):
    dma = pltpu.SemaphoreType.DMA
    return pl.pallas_call(
        kernel,
        out_shape=jax.ShapeDtypeStruct((2 * PK, 2, 2), F32),
        in_specs=[pl.BlockSpec(memory_space=pl.ANY)] * 2,
        out_specs=pl.BlockSpec(memory_space=pltpu.VMEM),
        scratch_shapes=[
            pltpu.VMEM((2, BL, HALF), BF16),
            pltpu.VMEM((2, BL, HALF), BF16),
            pltpu.VMEM((ROWS, HALF), F32),
            pltpu.VMEM((PK, BL, NX * SLAB), BF16),
            pltpu.VMEM((PK, BL, NX * SLAB), BF16),
            pltpu.VMEM((TROWS, SLAB), F32),
            pltpu.VMEM((NX, TROWS, SLAB), BF16),
            pltpu.VMEM((2, NZ, PADDED, CHUNK), BF16),
            pltpu.VMEM((2, NX, ROWS, CHUNK), BF16),
            pltpu.VMEM((2, NX, PADDED, CHUNK), BF16),
            pltpu.VMEM((NX, 4, TROWS, 128), BF16),
            pltpu.VMEM((NZ, TROWS, 128), BF16),
            pltpu.VMEM((2, NX, 4, TROWS, 128), BF16),
            pltpu.VMEM((2, NZ, 2, TROWS, 128), BF16),
            pltpu.VMEM((4, 384, 128), BF16),
            pltpu.VMEM((2, 128, 128), BF16),
            pltpu.VMEM((4 * ROWS, 128), F32),
            pltpu.VMEM((2 * TROWS, 128), F32),
            pltpu.VMEM((16, 8, 128), F32),
            pltpu.VMEM((8, 16, 128), F32),
            pltpu.VMEM((8, 16, 128), F32),
            pltpu.VMEM((8, 16, 128), F32),
            dma((2,)),
            dma((2,)), dma((2,)),
            dma((2, NZ - 1)), dma((2, NZ - 1)),
            dma((2, NX - 1)), dma((2, NX - 1)),
            dma((2, NX - 1)), dma((2, NX - 1)),
            dma((2,)), dma((2,)),
            dma((NX,)), dma((NX,)),
            dma((NZ,)), dma((NZ,)),
            dma((NZ,)), dma((NZ,)),
            dma((NX,)), dma((NX,)),
            dma((2, NZ)), dma((2, NZ)),
            dma((3, 8)), dma((3, 8)),
        ],
        compiler_params=pltpu.CompilerParams(
            collective_id=0, has_side_effects=True, vmem_limit_bytes=48 * 1024 * 1024
        ),
        cost_estimate=pl.CostEstimate(flops=2_500_000_000, bytes_accessed=20_000_000, transcendentals=0),
    )(factors, amplitudes)


def solution(mesh):
    return jax.shard_map(
        shards,
        mesh=mesh,
        in_specs=(P(None, "blk", "aux"), P(None, "blk", None)),
        out_specs=P(),
        check_vma=False,
    )
```

```python
import jax
import jax.numpy as jnp
from jax import lax
from jax.experimental import pallas as pl
from jax.experimental.pallas import tpu as pltpu
from jax.sharding import PartitionSpec as P

MESH = pl.DeviceIdType.MESH
F32, BF16 = jnp.float32, jnp.bfloat16

NX, NZ, NL = 4, 8, 4
PAIRS = 8
BL = 28
W = 2 * BL
ROWS = 2 * W
TOP = ROWS - 64
HALF = 1280
CHUNK = HALF // 2
SLAB = NZ * 2 * W
TROWS = BL * PAIRS
WIN1 = (0, 128, 384, 512)
NT = (((1,), (1,)), ((), ()))
PEERS = 21
DEEP = 2


def dot(a, b):
    return jnp.dot(a, b, preferred_element_type=F32)


def one_hot(rows, columns, test):
    r = lax.broadcasted_iota(jnp.int32, (rows, columns), 0)
    c = lax.broadcasted_iota(jnp.int32, (rows, columns), 1)
    return jnp.where(test(r, c), 1.0, 0.0).astype(BF16)


class Ring:
    def __init__(self, n, pos, slot, device, send, recv):
        self.n, self.pos, self.slot, self.device, self.send, self.recv = n, pos, slot, device, send, recv
        self.steps = n - 1

    def copy(self, way, step, back):
        q = step % 2 if way == 0 else 1 - step % 2
        j = step // 2 + back
        block = lax.rem(self.pos + (self.n - j if way == 0 else j), self.n)
        ref = self.slot(q, block)
        to = lax.rem(self.pos + (1 if way == 0 else self.n - 1), self.n)
        return pltpu.make_async_remote_copy(
            src_ref=ref,
            dst_ref=ref,
            send_sem=self.send.at[way, step],
            recv_sem=self.recv.at[way, step],
            device_id=self.device(to),
            device_id_type=MESH,
        )

    def start(self, way, step):
        self.copy(way, step, 0).start()

    def step(self, step):
        for way in (0, 1):
            self.copy(way, step, 1).wait_recv()
            if step + 2 < self.steps:
                self.start(way, step + 2)

    def finish(self):
        for step in range(self.steps):
            for way in (0, 1):
                self.copy(way, step, 0).wait_send()


def kernel(
    f_hbm, t_hbm, out_ref,
    fm, fo, df, tm, zb, xh, xo, p1, v2, t1, t2, iscr, acc, red0, red1, red2,
    loc, cs, cr, zs, zr, xs, xr, os, orr, ys, yr, p1s, p1r, p2s, p2r, ls, lr, c1s, c1r, c2s, c2r, rs, rr,
):
    blk = lax.axis_index("blk")
    l = lax.axis_index("aux")
    k = lax.rem(blk, 2)
    h = lax.rem(lax.div(blk, 2), 2)
    z = lax.rem(lax.div(blk, 4), NZ)
    x = lax.div(blk, 4 * NZ)
    m = lax.rem(l, 2)

    def at(x_, z_, h_, k_, l_):
        return (((x_ * NZ + z_) * 2 + h_) * 2 + k_, l_)

    other_core = at(x, z, h, 1 - k, l)
    other_half = at(x, z, 1 - h, k, l)
    partner = at(x, z, h, k, l + 1 - 2 * m)

    def xk_peer(o):
        g = lax.rem(x * 2 + k + o, 8)
        return at(lax.div(g, 2), z, h, lax.rem(g, 2), l)

    def z_peer(o):
        return at(x, lax.rem(z + o, NZ), h, k, l)

    def y_peer(o):
        g = lax.rem(h * NL + l + o, 8)
        return at(x, z, lax.div(g, NL), k, lax.rem(g, NL))

    def remote(src, dst, send, recv, device):
        return pltpu.make_async_remote_copy(
            src_ref=src, dst_ref=dst, send_sem=send, recv_sem=recv, device_id=device, device_id_type=MESH
        )

    own_q = pl.multiple_of(k * HALF, 128)
    other_q = pl.multiple_of((1 - k) * HALF, 128)
    load_t = pltpu.make_async_copy(t_hbm, tm, loc.at[1])
    load_f = pltpu.make_async_copy(f_hbm.at[:, :, pl.ds(own_q, HALF)], fm, loc.at[0])
    load_t.start()
    load_f.start()

    barrier = pltpu.get_barrier_semaphore()
    for o in range(1, 8):
        for peer in (xk_peer(o), z_peer(o), y_peer(o)):
            pl.semaphore_signal(barrier, inc=1, device_id=peer, device_id_type=MESH)

    load_t.wait()
    for i in range(4):
        pick = one_hot(
            384, 128, lambda r, c: ((c % 64) < W) & (r == (2 * i + c // 64) * 2 * W + h * W + c % 64 - WIN1[i])
        )
        for s in range(NX):
            first = s * SLAB + WIN1[i]
            p1[s, i] = dot(tm[:, first : first + 384], pick).astype(BF16)
    for i in range(NZ):
        first = min(128 * (i * 2 * W // 128), SLAB - 256)
        base = i * 2 * W - first
        low = one_hot(256, 128, lambda r, c: (c < W) & (r == base + (1 - h) * W + c))
        high = one_hot(256, 128, lambda r, c: (c >= 64) & (c < 64 + W) & (r == base + (1 - h) * W + c - 64))
        low_at = pl.multiple_of(2 * m * SLAB + first, 128)
        high_at = pl.multiple_of((2 * m + 1) * SLAB + first, 128)
        v2[i] = (dot(tm[:, pl.ds(low_at, 256)], low) + dot(tm[:, pl.ds(high_at, 256)], high)).astype(BF16)
    t1[k, x] = p1[x]
    t2[k, z, m] = v2[z]

    acc[...] = jnp.zeros_like(acc)
    load_f.wait()
    for i in range(BL):
        row = fm[i].astype(F32)
        for a in range(2):
            df[pl.ds(a * W + k * BL + i, 1), :] = row[a : a + 1, :]

    pl.semaphore_wait(barrier, PEERS)

    swap_f = remote(f_hbm.at[:, :, pl.ds(other_q, HALF)], fo, cs.at[0], cr.at[0], other_core)
    swap_f.start()

    def send_p1(o):
        to_x = lax.rem(x + o, NX)
        return remote(p1.at[to_x], t1.at[k, x], p1s.at[o], p1r.at[o], at(to_x, z, h, k, l))

    def send_p2(o):
        to_z = lax.rem(z + o, NZ)
        return remote(v2.at[to_z], t2.at[k, z, m], p2s.at[o], p2r.at[o], at(x, to_z, h, k, l))

    def t1_forward(o):
        ref = t1.at[k, lax.rem(x + NX - o, NX)]
        return remote(ref, ref, c1s.at[o], c1r.at[o], other_core)

    def t1_arrived(o):
        ref = t1.at[1 - k, lax.rem(x + NX - o, NX)]
        return remote(ref, ref, c1s.at[o], c1r.at[o], other_core)

    def p1_arrived(o):
        ref = t1.at[k, lax.rem(x + NX - o, NX)]
        return remote(ref, ref, p1s.at[o], p1r.at[o], other_core)

    def p2_arrived(o):
        ref = t2.at[k, lax.rem(z + NZ - o, NZ), m]
        return remote(ref, ref, p2s.at[o], p2r.at[o], other_core)

    def t2_share(o):
        ref = t2.at[k, lax.rem(z + NZ - o, NZ), m]
        return remote(ref, ref, ls.at[o], lr.at[o], partner)

    def share_arrived(o):
        ref = t2.at[k, lax.rem(z + NZ - o, NZ), 1 - m]
        return remote(ref, ref, ls.at[o], lr.at[o], partner)

    def t2_forward(o, part):
        ref = t2.at[k, lax.rem(z + NZ - o, NZ), m if part == 0 else 1 - m]
        return remote(ref, ref, c2s.at[part, o], c2r.at[part, o], other_core)

    def t2_arrived(o, part):
        ref = t2.at[1 - k, lax.rem(z + NZ - o, NZ), m if part == 0 else 1 - m]
        return remote(ref, ref, c2s.at[part, o], c2r.at[part, o], other_core)

    ring_z = Ring(NZ, z, lambda q, i: zb.at[q, i], lambda i: at(x, i, h, k, l), zs, zr)
    ring_x = Ring(NX, x, lambda q, i: xh.at[q, i], lambda i: at(i, z, h, k, l), xs, xr)
    ring_o = Ring(NX, x, lambda q, i: xo.at[q, i], lambda i: at(i, z, h, k, l), os, orr)

    def swap_y(q):
        return remote(xh.at[q, x], xo.at[q, x], ys.at[q], yr.at[q], other_half)

    swap_f.wait_recv()
    for i in range(BL):
        row = fo[i].astype(F32)
        for a in range(2):
            df[pl.ds(a * W + (1 - k) * BL + i, 1), :] = row[a : a + 1, :]
    for q in range(2):
        chunk = df[:, q * CHUNK : (q + 1) * CHUNK].astype(BF16)
        zb[q, z] = chunk
        xh[q, x] = chunk
    for step in range(2):
        for way in (0, 1):
            ring_z.start(way, step)
        for way in (0, 1):
            ring_x.start(way, step)
        swap_y(step).start()

    for o in range(1, NX):
        send_p1(o).start()
    for o in range(1, NZ):
        send_p2(o).start()
    t1_forward(0).start()
    t2_share(0).start()
    t2_forward(0, 0).start()

    def both(buf, q, pair):
        rows = [buf[q, 2 * pair + i, pl.ds(first, 64), :] for first in (0, TOP) for i in range(2)]
        return jnp.concatenate(rows, axis=0)

    def multiply(block, tiles, sums):
        parts = [[None] * 8 for _ in range(4)]
        for kk in range(2):
            low = tiles(kk).astype(F32)
            high = pltpu.roll(low, 8, 1)
            for i in range(BL):
                for a in range(2):
                    row = block * ROWS + a * W + kk * BL + i
                    for b, t in enumerate((low, high)):
                        term = iscr[b, pl.ds(row, 1), :] * t[PAIRS * i : PAIRS * (i + 1), :]
                        held, j = parts[2 * a + b], i % DEEP
                        held[j] = term if held[j] is None else held[j] + term
        return tuple(sums[n] + sum(parts[n][1:DEEP], parts[n][0]) for n in range(4))

    def add_up(work):
        sums = work(tuple(acc[n] for n in range(4)))
        for n in range(4):
            acc[n] = sums[n]

    def keep(integrals):
        for b in range(2):
            iscr[b] = integrals[:, 128 * b : 128 * (b + 1)]

    def own_half(pair):
        pair = lax.rem(pair, NZ // 2)
        total = 0.0
        for q in range(2):
            total += lax.dot_general(
                xh[q].reshape(NX * ROWS, CHUNK), both(zb, q, pair), NT, preferred_element_type=F32
            )
        keep(total)

        def body(b, sums):
            return multiply(b, lambda kk: t1[kk, b, pair], sums)

        add_up(lambda sums: lax.fori_loop(0, NX, body, sums))

    def cross_half(offsets):
        zis = [lax.rem(z + o, NZ) for o in offsets]

        def body(pair, sums):
            total = 0.0
            for q in range(2):
                rows = jnp.concatenate([zb[q, zi] for zi in zis], axis=0)
                total += lax.dot_general(rows, both(xo, q, pair), NT, preferred_element_type=F32)
            keep(total)
            for i, zi in enumerate(zis):
                sums = multiply(i, lambda kk: t2[kk, zi, pair], sums)
            return sums

        add_up(lambda sums: lax.fori_loop(0, NX // 2, body, sums))

    here = lax.div(z, 2)
    turn = 1 - 2 * lax.rem(z, 2)

    def pass_x():
        for o in range(1, NX):
            p1_arrived(o).wait_recv()
            t1_forward(o).start()

    def pass_z():
        def pass_on(o, _):
            p2_arrived(o).wait_recv()
            t2_share(o).start()
            t2_forward(o, 0).start()
            return 0

        lax.fori_loop(1, NZ, pass_on, 0)

    def pass_shared():
        def pass_on(o, _):
            share_arrived(o).wait_recv()
            t2_forward(o, 1).start()
            return 0

        lax.fori_loop(0, NZ, pass_on, 0)

    def settle_x():
        for o in range(NX):
            t1_arrived(o).wait_recv()

    def settle_z():
        def settle(o, _):
            t2_arrived(o, 0).wait_recv()
            t2_arrived(o, 1).wait_recv()
            return 0

        lax.fori_loop(0, NZ, settle, 0)

    def swapped(q):
        swap_y(q).wait_recv()
        ring_o.start(0, q)
        ring_o.start(1, 1 - q)

    ring_z.step(0)
    ring_x.step(0)
    ring_z.step(1)
    ring_x.step(1)
    ring_x.step(2)
    ring_z.step(2)
    swapped(0)
    pass_x()
    ring_z.step(3)
    swapped(1)
    settle_x()
    own_half(here)
    pass_z()
    ring_z.step(4)
    ring_o.step(0)
    own_half(here + 4 - turn)
    pass_shared()
    ring_z.step(5)
    ring_o.step(1)
    own_half(here + 4 + turn)
    settle_z()
    ring_o.step(2)
    cross_half((0, 1, 7, 2))
    ring_z.step(6)
    own_half(here + 2)
    cross_half((6, 3, 5, 4))

    lane = lax.broadcasted_iota(jnp.int32, (PAIRS, 128), 1)
    total = jnp.zeros((PAIRS, 128), F32)
    for n in range(4):
        total = jnp.where(lane == n, jnp.sum(acc[n], axis=1, keepdims=True), total)
    rounds = ((red0, x * 2 + k, xk_peer), (red1, z, z_peer), (red2, h * NL + l, y_peer))
    for i, (held, me, peer) in enumerate(rounds):
        held[me] = total
        for o in range(1, 8):
            remote(held.at[me], held.at[me], rs.at[i, o], rr.at[i, o], peer(o)).start()
        for o in range(1, 8):
            ref = held.at[lax.rem(me + 8 - o, 8)]
            remote(ref, ref, rs.at[i, o], rr.at[i, o], peer(o)).wait_recv()
        total = held[0]
        for o in range(1, 8):
            total = total + held[o]
    diagonal = lax.broadcasted_iota(jnp.int32, (PAIRS, PAIRS), 0) == lax.broadcasted_iota(
        jnp.int32, (PAIRS, PAIRS), 1
    )
    for a in range(2):
        for b in range(2):
            column = total[:, 2 * a + b : 2 * a + b + 1]
            out_ref[a, pl.ds(b, 1), :] = jnp.sum(jnp.where(diagonal, column, 0.0), axis=0, keepdims=True)

    swap_f.wait_send()
    ring_z.finish()
    ring_x.finish()
    ring_o.finish()
    for q in range(2):
        swap_y(q).wait_send()
    for o in range(1, NX):
        send_p1(o).wait_send()
    for o in range(NX):
        t1_forward(o).wait_send()
    for o in range(1, NZ):
        send_p2(o).wait_send()
    for o in range(NZ):
        t2_share(o).wait_send()
        t2_forward(o, 0).wait_send()
        t2_forward(o, 1).wait_send()
    for i, (held, me, peer) in enumerate(rounds):
        for o in range(1, 8):
            remote(held.at[me], held.at[me], rs.at[i, o], rr.at[i, o], peer(o)).wait_send()


def shards(factors, amplitudes):
    dma = pltpu.SemaphoreType.DMA
    by_orbital = jnp.transpose(amplitudes, (1, 0, 2)).reshape(TROWS, NX * SLAB)
    out = pl.pallas_call(
        kernel,
        out_shape=jax.ShapeDtypeStruct((2, 2, PAIRS), F32),
        in_specs=[pl.BlockSpec(memory_space=pl.ANY)] * 2,
        out_specs=pl.BlockSpec(memory_space=pltpu.VMEM),
        scratch_shapes=[
            pltpu.VMEM((BL, 2, HALF), BF16),
            pltpu.VMEM((BL, 2, HALF), BF16),
            pltpu.VMEM((ROWS, HALF), F32),
            pltpu.VMEM((TROWS, NX * SLAB), BF16),
            pltpu.VMEM((2, NZ, ROWS, CHUNK), BF16),
            pltpu.VMEM((2, NX, ROWS, CHUNK), BF16),
            pltpu.VMEM((2, NX, ROWS, CHUNK), BF16),
            pltpu.VMEM((NX, 4, TROWS, 128), BF16),
            pltpu.VMEM((NZ, TROWS, 128), BF16),
            pltpu.VMEM((2, NX, 4, TROWS, 128), BF16),
            pltpu.VMEM((2, NZ, 2, TROWS, 128), BF16),
            pltpu.VMEM((2, 4 * ROWS, 128), F32),
            pltpu.VMEM((4, PAIRS, 128), F32),
            pltpu.VMEM((8, PAIRS, 128), F32),
            pltpu.VMEM((8, PAIRS, 128), F32),
            pltpu.VMEM((8, PAIRS, 128), F32),
            dma((2,)),
            dma((2,)), dma((2,)),
            dma((2, NZ - 1)), dma((2, NZ - 1)),
            dma((2, NX - 1)), dma((2, NX - 1)),
            dma((2, NX - 1)), dma((2, NX - 1)),
            dma((2,)), dma((2,)),
            dma((NX,)), dma((NX,)),
            dma((NZ,)), dma((NZ,)),
            dma((NZ,)), dma((NZ,)),
            dma((NX,)), dma((NX,)),
            dma((2, NZ)), dma((2, NZ)),
            dma((3, 8)), dma((3, 8)),
        ],
        compiler_params=pltpu.CompilerParams(
            collective_id=0, has_side_effects=True, vmem_limit_bytes=62 * 1024 * 1024
        ),
        cost_estimate=pl.CostEstimate(flops=2_500_000_000, bytes_accessed=20_000_000, transcendentals=0),
    )(jnp.transpose(factors, (1, 0, 2)), by_orbital)
    return jnp.transpose(out, (2, 0, 1))


def solution(mesh):
    return jax.shard_map(
        shards,
        mesh=mesh,
        in_specs=(P(None, "blk", "aux"), P(None, "blk", None)),
        out_specs=P(),
        check_vma=False,
    )
```

```python
import jax
import jax.numpy as jnp
from jax import lax
from jax.experimental import pallas as pl
from jax.experimental.pallas import tpu as pltpu
from jax.sharding import PartitionSpec as P

MESH = pl.DeviceIdType.MESH
F32, BF16 = jnp.float32, jnp.bfloat16

NX, NZ, NL = 4, 8, 4
PAIRS = 8
BL = 28
W = 2 * BL
ROWS = 2 * W
TOP = ROWS - 64
HALF = 1280
CHUNK = HALF // 2
SLAB = NZ * 2 * W
TROWS = BL * PAIRS
WIN1 = (0, 128, 384, 512)
NT = (((1,), (1,)), ((), ()))
PEERS = 21
DEEP = 2


def dot(a, b):
    return jnp.dot(a, b, preferred_element_type=F32)


def one_hot(rows, columns, test):
    r = lax.broadcasted_iota(jnp.int32, (rows, columns), 0)
    c = lax.broadcasted_iota(jnp.int32, (rows, columns), 1)
    return jnp.where(test(r, c), 1.0, 0.0).astype(BF16)


class Ring:
    def __init__(self, n, pos, slot, device, send, recv):
        self.n, self.pos, self.slot, self.device, self.send, self.recv = n, pos, slot, device, send, recv
        self.steps = n - 1

    def copy(self, way, step, back):
        q = step % 2 if way == 0 else 1 - step % 2
        j = step // 2 + back
        block = lax.rem(self.pos + (self.n - j if way == 0 else j), self.n)
        ref = self.slot(q, block)
        to = lax.rem(self.pos + (1 if way == 0 else self.n - 1), self.n)
        return pltpu.make_async_remote_copy(
            src_ref=ref,
            dst_ref=ref,
            send_sem=self.send.at[way, step],
            recv_sem=self.recv.at[way, step],
            device_id=self.device(to),
            device_id_type=MESH,
        )

    def start(self, way, step):
        self.copy(way, step, 0).start()

    def step(self, step):
        for way in (0, 1):
            self.copy(way, step, 1).wait_recv()
            if step + 2 < self.steps:
                self.start(way, step + 2)

    def finish(self):
        for step in range(self.steps):
            for way in (0, 1):
                self.copy(way, step, 0).wait_send()


def kernel(
    f_hbm, t_hbm, out_ref,
    fm, fo, df, tm, zb, xh, xo, p1, v2, t1, t2, iscr, acc, red0, red1, red2,
    loc, cs, cr, zs, zr, xs, xr, os, orr, ys, yr, p1s, p1r, p2s, p2r, ls, lr, c1s, c1r, c2s, c2r, rs, rr,
):
    blk = lax.axis_index("blk")
    l = lax.axis_index("aux")
    k = lax.rem(blk, 2)
    h = lax.rem(lax.div(blk, 2), 2)
    z = lax.rem(lax.div(blk, 4), NZ)
    x = lax.div(blk, 4 * NZ)
    m = lax.rem(l, 2)

    def at(x_, z_, h_, k_, l_):
        return (((x_ * NZ + z_) * 2 + h_) * 2 + k_, l_)

    other_core = at(x, z, h, 1 - k, l)
    other_half = at(x, z, 1 - h, k, l)
    partner = at(x, z, h, k, l + 1 - 2 * m)

    def xk_peer(o):
        g = lax.rem(x * 2 + k + o, 8)
        return at(lax.div(g, 2), z, h, lax.rem(g, 2), l)

    def z_peer(o):
        return at(x, lax.rem(z + o, NZ), h, k, l)

    def y_peer(o):
        g = lax.rem(h * NL + l + o, 8)
        return at(x, z, lax.div(g, NL), k, lax.rem(g, NL))

    def remote(src, dst, send, recv, device):
        return pltpu.make_async_remote_copy(
            src_ref=src, dst_ref=dst, send_sem=send, recv_sem=recv, device_id=device, device_id_type=MESH
        )

    own_q = pl.multiple_of(k * HALF, 128)
    other_q = pl.multiple_of((1 - k) * HALF, 128)
    load_t = pltpu.make_async_copy(t_hbm, tm, loc.at[1])
    load_f = pltpu.make_async_copy(f_hbm.at[:, :, pl.ds(own_q, HALF)], fm, loc.at[0])
    load_t.start()
    load_f.start()

    barrier = pltpu.get_barrier_semaphore()
    for o in range(1, 8):
        for peer in (xk_peer(o), z_peer(o), y_peer(o)):
            pl.semaphore_signal(barrier, inc=1, device_id=peer, device_id_type=MESH)

    load_t.wait()
    for i in range(4):
        pick = one_hot(
            384, 128, lambda r, c: ((c % 64) < W) & (r == (2 * i + c // 64) * 2 * W + h * W + c % 64 - WIN1[i])
        )
        for s in range(NX):
            first = s * SLAB + WIN1[i]
            p1[s, i] = dot(tm[:, first : first + 384], pick).astype(BF16)
    for i in range(NZ):
        first = min(128 * (i * 2 * W // 128), SLAB - 256)
        base = i * 2 * W - first
        low = one_hot(256, 128, lambda r, c: (c < W) & (r == base + (1 - h) * W + c))
        high = one_hot(256, 128, lambda r, c: (c >= 64) & (c < 64 + W) & (r == base + (1 - h) * W + c - 64))
        low_at = pl.multiple_of(2 * m * SLAB + first, 128)
        high_at = pl.multiple_of((2 * m + 1) * SLAB + first, 128)
        v2[i] = (dot(tm[:, pl.ds(low_at, 256)], low) + dot(tm[:, pl.ds(high_at, 256)], high)).astype(BF16)
    t1[k, x] = p1[x]
    t2[k, z, m] = v2[z]

    acc[...] = jnp.zeros_like(acc)
    load_f.wait()
    for i in range(BL):
        row = fm[i].astype(F32)
        for a in range(2):
            df[pl.ds(a * W + k * BL + i, 1), :] = row[a : a + 1, :]

    pl.semaphore_wait(barrier, PEERS)

    swap_f = remote(f_hbm.at[:, :, pl.ds(other_q, HALF)], fo, cs.at[0], cr.at[0], other_core)
    swap_f.start()

    def send_p1(o):
        to_x = lax.rem(x + o, NX)
        return remote(p1.at[to_x], t1.at[k, x], p1s.at[o], p1r.at[o], at(to_x, z, h, k, l))

    def send_p2(o):
        to_z = lax.rem(z + o, NZ)
        return remote(v2.at[to_z], t2.at[k, z, m], p2s.at[o], p2r.at[o], at(x, to_z, h, k, l))

    def t1_forward(o):
        ref = t1.at[k, lax.rem(x + NX - o, NX)]
        return remote(ref, ref, c1s.at[o], c1r.at[o], other_core)

    def t1_arrived(o):
        ref = t1.at[1 - k, lax.rem(x + NX - o, NX)]
        return remote(ref, ref, c1s.at[o], c1r.at[o], other_core)

    def p1_arrived(o):
        ref = t1.at[k, lax.rem(x + NX - o, NX)]
        return remote(ref, ref, p1s.at[o], p1r.at[o], other_core)

    def p2_arrived(o):
        ref = t2.at[k, lax.rem(z + NZ - o, NZ), m]
        return remote(ref, ref, p2s.at[o], p2r.at[o], other_core)

    def t2_share(o):
        ref = t2.at[k, lax.rem(z + NZ - o, NZ), m]
        return remote(ref, ref, ls.at[o], lr.at[o], partner)

    def share_arrived(o):
        ref = t2.at[k, lax.rem(z + NZ - o, NZ), 1 - m]
        return remote(ref, ref, ls.at[o], lr.at[o], partner)

    def t2_forward(o, part):
        ref = t2.at[k, lax.rem(z + NZ - o, NZ), m if part == 0 else 1 - m]
        return remote(ref, ref, c2s.at[part, o], c2r.at[part, o], other_core)

    def t2_arrived(o, part):
        ref = t2.at[1 - k, lax.rem(z + NZ - o, NZ), m if part == 0 else 1 - m]
        return remote(ref, ref, c2s.at[part, o], c2r.at[part, o], other_core)

    ring_z = Ring(NZ, z, lambda q, i: zb.at[q, i], lambda i: at(x, i, h, k, l), zs, zr)
    ring_x = Ring(NX, x, lambda q, i: xh.at[q, i], lambda i: at(i, z, h, k, l), xs, xr)
    ring_o = Ring(NX, x, lambda q, i: xo.at[q, i], lambda i: at(i, z, h, k, l), os, orr)

    def swap_y(q):
        return remote(xh.at[q, x], xo.at[q, x], ys.at[q], yr.at[q], other_half)

    for o in range(1, NX):
        send_p1(o).start()
    for o in range(1, NZ):
        send_p2(o).start()
    t1_forward(0).start()
    t2_share(0).start()
    t2_forward(0, 0).start()
    swap_f.wait_recv()
    for i in range(BL):
        row = fo[i].astype(F32)
        for a in range(2):
            df[pl.ds(a * W + (1 - k) * BL + i, 1), :] = row[a : a + 1, :]
    for q in range(2):
        chunk = df[:, q * CHUNK : (q + 1) * CHUNK].astype(BF16)
        zb[q, z] = chunk
        xh[q, x] = chunk
    for step in range(2):
        for way in (0, 1):
            ring_z.start(way, step)
        for way in (0, 1):
            ring_x.start(way, step)
        swap_y(step).start()


    def both(buf, q, pair):
        rows = [buf[q, 2 * pair + i, pl.ds(first, 64), :] for first in (0, TOP) for i in range(2)]
        return jnp.concatenate(rows, axis=0)

    def multiply(block, tiles, sums):
        parts = [[None] * 8 for _ in range(4)]
        for kk in range(2):
            low = tiles(kk).astype(F32)
            high = pltpu.roll(low, 8, 1)
            for i in range(BL):
                for a in range(2):
                    row = block * ROWS + a * W + kk * BL + i
                    for b, t in enumerate((low, high)):
                        term = iscr[b, pl.ds(row, 1), :] * t[PAIRS * i : PAIRS * (i + 1), :]
                        held, j = parts[2 * a + b], i % DEEP
                        held[j] = term if held[j] is None else held[j] + term
        return tuple(sums[n] + sum(parts[n][1:DEEP], parts[n][0]) for n in range(4))

    def add_up(work):
        sums = work(tuple(acc[n] for n in range(4)))
        for n in range(4):
            acc[n] = sums[n]

    def keep(integrals):
        for b in range(2):
            iscr[b, pl.ds(0, integrals.shape[0]), :] = integrals[:, 128 * b : 128 * (b + 1)]

    def own_half(pair):
        pair = lax.rem(pair, NZ // 2)
        total = 0.0
        for q in range(2):
            total += lax.dot_general(
                xh[q].reshape(NX * ROWS, CHUNK), both(zb, q, pair), NT, preferred_element_type=F32
            )
        keep(total)

        def body(b, sums):
            return multiply(b, lambda kk: t1[kk, b, pair], sums)

        add_up(lambda sums: lax.fori_loop(0, NX, body, sums))

    def cross_half(offsets):
        zis = [lax.rem(z + o, NZ) for o in offsets]

        def body(pair, sums):
            total = 0.0
            for q in range(2):
                rows = jnp.concatenate([zb[q, zi] for zi in zis], axis=0)
                total += lax.dot_general(rows, both(xo, q, pair), NT, preferred_element_type=F32)
            keep(total)
            for i, zi in enumerate(zis):
                sums = multiply(i, lambda kk: t2[kk, zi, pair], sums)
            return sums

        add_up(lambda sums: lax.fori_loop(0, NX // 2, body, sums))

    here = lax.div(z, 2)
    turn = 1 - 2 * lax.rem(z, 2)

    def pass_x():
        for o in range(1, NX):
            p1_arrived(o).wait_recv()
            t1_forward(o).start()

    def pass_z():
        def pass_on(o, _):
            p2_arrived(o).wait_recv()
            t2_share(o).start()
            t2_forward(o, 0).start()
            return 0

        lax.fori_loop(1, NZ, pass_on, 0)

    def pass_shared():
        def pass_on(o, _):
            share_arrived(o).wait_recv()
            t2_forward(o, 1).start()
            return 0

        lax.fori_loop(0, NZ, pass_on, 0)

    def settle_x():
        for o in range(NX):
            t1_arrived(o).wait_recv()

    def settle_z():
        def settle(o, _):
            t2_arrived(o, 0).wait_recv()
            t2_arrived(o, 1).wait_recv()
            return 0

        lax.fori_loop(0, NZ, settle, 0)

    def swapped(q):
        swap_y(q).wait_recv()
        ring_o.start(0, q)
        ring_o.start(1, 1 - q)

    ring_x.step(0)
    ring_z.step(0)
    ring_x.step(1)
    ring_z.step(1)
    pass_x()
    ring_x.step(2)
    swapped(0)
    ring_z.step(2)
    pass_z()
    swapped(1)
    ring_z.step(3)
    settle_x()
    own_half(here)
    ring_z.step(4)
    ring_o.step(0)
    pass_shared()
    own_half(here + 4 - turn)
    ring_o.step(1)
    ring_z.step(5)
    settle_z()
    own_half(here + 4 + turn)
    ring_o.step(2)
    cross_half((0, 1, 7, 2))
    cross_half((6, 3, 5))
    ring_z.step(6)
    own_half(here + 2)
    cross_half((4,))

    lane = lax.broadcasted_iota(jnp.int32, (PAIRS, 128), 1)
    total = jnp.zeros((PAIRS, 128), F32)
    for n in range(4):
        total = jnp.where(lane == n, jnp.sum(acc[n], axis=1, keepdims=True), total)
    rounds = ((red0, x * 2 + k, xk_peer), (red1, z, z_peer), (red2, h * NL + l, y_peer))
    for i, (held, me, peer) in enumerate(rounds):
        held[me] = total
        for o in range(1, 8):
            remote(held.at[me], held.at[me], rs.at[i, o], rr.at[i, o], peer(o)).start()
        for o in range(1, 8):
            ref = held.at[lax.rem(me + 8 - o, 8)]
            remote(ref, ref, rs.at[i, o], rr.at[i, o], peer(o)).wait_recv()
        total = held[0]
        for o in range(1, 8):
            total = total + held[o]
    diagonal = lax.broadcasted_iota(jnp.int32, (PAIRS, PAIRS), 0) == lax.broadcasted_iota(
        jnp.int32, (PAIRS, PAIRS), 1
    )
    for a in range(2):
        for b in range(2):
            column = total[:, 2 * a + b : 2 * a + b + 1]
            out_ref[a, pl.ds(b, 1), :] = jnp.sum(jnp.where(diagonal, column, 0.0), axis=0, keepdims=True)

    swap_f.wait_send()
    ring_z.finish()
    ring_x.finish()
    ring_o.finish()
    for q in range(2):
        swap_y(q).wait_send()
    for o in range(1, NX):
        send_p1(o).wait_send()
    for o in range(NX):
        t1_forward(o).wait_send()
    for o in range(1, NZ):
        send_p2(o).wait_send()
    for o in range(NZ):
        t2_share(o).wait_send()
        t2_forward(o, 0).wait_send()
        t2_forward(o, 1).wait_send()
    for i, (held, me, peer) in enumerate(rounds):
        for o in range(1, 8):
            remote(held.at[me], held.at[me], rs.at[i, o], rr.at[i, o], peer(o)).wait_send()


def shards(factors, amplitudes):
    dma = pltpu.SemaphoreType.DMA
    by_orbital = jnp.transpose(amplitudes, (1, 0, 2)).reshape(TROWS, NX * SLAB)
    out = pl.pallas_call(
        kernel,
        out_shape=jax.ShapeDtypeStruct((2, 2, PAIRS), F32),
        in_specs=[pl.BlockSpec(memory_space=pl.ANY)] * 2,
        out_specs=pl.BlockSpec(memory_space=pltpu.VMEM),
        scratch_shapes=[
            pltpu.VMEM((BL, 2, HALF), BF16),
            pltpu.VMEM((BL, 2, HALF), BF16),
            pltpu.VMEM((ROWS, HALF), F32),
            pltpu.VMEM((TROWS, NX * SLAB), BF16),
            pltpu.VMEM((2, NZ, ROWS, CHUNK), BF16),
            pltpu.VMEM((2, NX, ROWS, CHUNK), BF16),
            pltpu.VMEM((2, NX, ROWS, CHUNK), BF16),
            pltpu.VMEM((NX, 4, TROWS, 128), BF16),
            pltpu.VMEM((NZ, TROWS, 128), BF16),
            pltpu.VMEM((2, NX, 4, TROWS, 128), BF16),
            pltpu.VMEM((2, NZ, 2, TROWS, 128), BF16),
            pltpu.VMEM((2, 4 * ROWS, 128), F32),
            pltpu.VMEM((4, PAIRS, 128), F32),
            pltpu.VMEM((8, PAIRS, 128), F32),
            pltpu.VMEM((8, PAIRS, 128), F32),
            pltpu.VMEM((8, PAIRS, 128), F32),
            dma((2,)),
            dma((2,)), dma((2,)),
            dma((2, NZ - 1)), dma((2, NZ - 1)),
            dma((2, NX - 1)), dma((2, NX - 1)),
            dma((2, NX - 1)), dma((2, NX - 1)),
            dma((2,)), dma((2,)),
            dma((NX,)), dma((NX,)),
            dma((NZ,)), dma((NZ,)),
            dma((NZ,)), dma((NZ,)),
            dma((NX,)), dma((NX,)),
            dma((2, NZ)), dma((2, NZ)),
            dma((3, 8)), dma((3, 8)),
        ],
        compiler_params=pltpu.CompilerParams(
            collective_id=0, has_side_effects=True, vmem_limit_bytes=62 * 1024 * 1024
        ),
        cost_estimate=pl.CostEstimate(flops=2_500_000_000, bytes_accessed=20_000_000, transcendentals=0),
    )(jnp.transpose(factors, (1, 0, 2)), by_orbital)
    return jnp.transpose(out, (2, 0, 1))


def solution(mesh):
    return jax.shard_map(
        shards,
        mesh=mesh,
        in_specs=(P(None, "blk", "aux"), P(None, "blk", None)),
        out_specs=P(),
        check_vma=False,
    )
```
